32 devices in a mesh: dp: 4 (over x, core), tensor: 8 (over z, y).
Axes of the slice: x: 2, y: 2, z: 4, core: 2. Of those that a mesh axis runs over, the one named last changes fastest.
Arguments:
- tokens: bfloat16 [2048, 4096], P(('dp', 'tensor')), may hold values from -6 to 6
- cotangent: bfloat16 [2048, 4096], P(('dp', 'tensor')), may hold values from -12 to 12
- loss_mask: int32 [2048], P(('dp', 'tensor')), may hold values from 0 to 1, as said below
- gate_weight: bfloat16 [4096, 14336], P(None, 'tensor'), may hold values from -0.09375 to 0.09375
- up_weight: bfloat16 [4096, 14336], P(None, 'tensor'), may hold values from -0.09375 to 0.09375
- down_weight: bfloat16 [14336, 4096], P('tensor'), may hold values from -0.046875 to 0.046875
- probe_seed: int32 [1], replicated, may hold values from 0 to 1048575
Outputs:
- diag_gate: float32 [4096, 14336], P('dp', 'tensor')
The draws below stay inside these ranges and needn't reach their ends.
Inputs may be any that keep to these rules, and one draw needn't show every extreme that they name: `loss_mask`: 0 or 1; the first entry is 1.
All inputs are finite; a program needn't handle non-finite values.
Results may differ from the reference program's by a relative error of at most 0.0029.
Values may be sent and summed in bfloat16 or wider, within the bound.
No kernel may reach another device: no remote copies, remote signals or barrier semaphores. Data moves between devices by JAX's collectives and lax.ppermute only.
A program may use at most 192 MiB of HBM per device.

```python
import jax
import jax.numpy as jnp
from jax import lax

D = 4096
FF = 14336
TOK_REP = 512
TOKENS = 2048
N_DP = 4


def draw_loss_mask(key, part):
    key = jax.random.fold_in(key, 7)
    position = jnp.arange(TOKENS, dtype=jnp.int32)
    threshold = 64 + 128 * position // TOKENS
    ticket = jax.random.randint(key, (TOKENS,), 0, 256, dtype=jnp.int32)
    live_flags = jnp.where(ticket < threshold, 1, 0).astype(jnp.int32)
    return jnp.where(position == 0, 1, live_flags).astype(jnp.int32)


def steps_of(stream_key, extent, cuts, low, high):
    factor_of = 1.0
    for axis_at, shards_of in cuts:
        heights = jax.random.uniform(jax.random.fold_in(jax.random.fold_in(stream_key, 6), axis_at), (shards_of,), jnp.float32, low / len(cuts), high / len(cuts))
        factor_of = factor_of * jnp.repeat(jnp.exp(heights), extent[axis_at] // shards_of).reshape((-1,) + (1,) * (len(extent) - 1 - axis_at))
    return factor_of


def centred(rng, dims, width, reach, shards=(), kind=jnp.bfloat16):
    result = width * jax.random.normal(rng, dims, jnp.float32)
    if shards:
        result = result * steps_of(rng, dims, shards, -0.22, 0.18)
    return jnp.clip(result, -reach, reach).astype(kind)


def setup_inputs(seed: int = 0) -> dict:
    key_of = jax.random.split(jax.random.key(seed), 8)
    tokens = centred(key_of[0], (TOKENS, D), 1.0, 6.0, ((0, 32),))
    cotangent = centred(key_of[1], (TOKENS, D), 3.0, 12.0, ((0, 32),))
    loss_mask = draw_loss_mask(jax.random.fold_in(key_of[7], 71), 0)
    gate_weight = centred(key_of[3], (D, FF), D ** -0.5, 0.09375, ((1, 8),))
    up_weight = centred(key_of[4], (D, FF), D ** -0.5, 0.09375, ((1, 8),))
    down_weight = centred(key_of[5], (FF, D), FF ** -0.5, 0.046875, ((0, 8),))
    probe_seed = jax.random.randint(key_of[6], (1,), 0, 1048576).astype(jnp.int32)
    return {"tokens": tokens, "cotangent": cotangent, "loss_mask": loss_mask, "gate_weight": gate_weight, "up_weight": up_weight, "down_weight": down_weight, "probe_seed": probe_seed}


def probe_signs(seed_value, row_count, col_count, first_col, full_width):
    row_index = lax.broadcasted_iota(jnp.int32, (row_count, col_count), 0)
    col_index = lax.broadcasted_iota(jnp.int32, (row_count, col_count), 1) + first_col
    hashed = (row_index * full_width + col_index) * jnp.int32(-1640531535) + seed_value * jnp.int32(668265263)
    hashed = hashed ^ lax.shift_right_logical(hashed, jnp.full_like(hashed, 15))
    hashed = hashed * jnp.int32(739982445)
    hashed = hashed ^ lax.shift_right_logical(hashed, jnp.full_like(hashed, 12))
    hashed = hashed * jnp.int32(695872825)
    hashed = hashed ^ lax.shift_right_logical(hashed, jnp.full_like(hashed, 15))
    lowbit = lax.shift_right_logical(hashed, jnp.full_like(hashed, 16)) & jnp.int32(1)
    return jnp.int32(1) - jnp.int32(2) * lowbit


def curvature(gate_pre):
    sigmoid_val = jax.nn.sigmoid(gate_pre)
    return sigmoid_val * (1.0 - sigmoid_val) * (2.0 + gate_pre * (1.0 - 2.0 * sigmoid_val))


def reference(tokens, cotangent, loss_mask, gate_weight, up_weight, down_weight, probe_seed):
    sign_table = probe_signs(probe_seed[0], D, FF, jnp.int32(0), FF)
    probe_bf = sign_table.astype(jnp.bfloat16)
    live_flags = loss_mask.astype(jnp.float32)
    live_count = jnp.sum(live_flags)
    masked = (cotangent.astype(jnp.float32) * live_flags[:, None]).astype(jnp.bfloat16)
    token_blocks = tokens.reshape(N_DP, TOK_REP, D)
    masked_blocks = masked.reshape(N_DP, TOK_REP, D)

    def replica_step(running, block_pair):
        features, masked_rows = block_pair
        gate_pre = jnp.dot(features, gate_weight, preferred_element_type=jnp.float32)
        up_proj = jnp.dot(features, up_weight, preferred_element_type=jnp.float32)
        tangent = jnp.dot(features, probe_bf, preferred_element_type=jnp.float32)
        back_grad = jnp.dot(masked_rows, down_weight.T, preferred_element_type=jnp.float32)
        operand = (back_grad * up_proj * curvature(gate_pre) * tangent).astype(jnp.bfloat16)
        return running + jnp.dot(features.T, operand, preferred_element_type=jnp.float32), None

    total_sum, unused = lax.scan(replica_step, jnp.zeros((D, FF), jnp.float32), (token_blocks, masked_blocks))
    hessian = total_sum / live_count
    return sign_table.astype(jnp.float32) * hessian
```

```python
import functools

import jax
import jax.numpy as jnp
from jax import lax
from jax.experimental import pallas as pl
from jax.experimental.pallas import tpu as pltpu
from jax.sharding import PartitionSpec as P

FF = 14336
MULT = -1640531535

contract_rows = (((0,), (0,)), ((), ()))
contract_last = (((1,), (1,)), ((), ()))

anywhere = pl.BlockSpec(memory_space=pl.ANY)
in_smem = pl.BlockSpec(memory_space=pltpu.SMEM)
params = pltpu.CompilerParams(vmem_limit_bytes=40 * 1024 * 1024)


def cost(flops, moved):
    return pl.CostEstimate(flops=int(flops), bytes_accessed=int(moved), transcendentals=0)


def mixed_sign(hashed):
    hashed = hashed ^ lax.shift_right_logical(hashed, jnp.full_like(hashed, 15))
    hashed = hashed * jnp.int32(739982445)
    hashed = hashed ^ lax.shift_right_logical(hashed, jnp.full_like(hashed, 12))
    hashed = hashed * jnp.int32(695872825)
    return (hashed ^ lax.shift_left(hashed, jnp.full_like(hashed, 15))) < 0


def column_block(width):
    return 256 if width % 256 == 0 else width


def sign_kernel(start_row, seed_and_col, *rest):
    out = rest[-1]
    rows, width = out.shape
    first = start_row + pl.program_id(0) * rows
    col = lax.broadcasted_iota(jnp.int32, (16, width), 1) + seed_and_col[1]
    row = lax.broadcasted_iota(jnp.int32, (16, width), 0)
    base = (row * FF + col) * jnp.int32(MULT) + seed_and_col[0] * jnp.int32(668265263)

    def chunk(c, carry):
        at = pl.multiple_of(c * 16, 16)
        hashed = base + (first + at) * (jnp.int32(FF) * jnp.int32(MULT))
        out[pl.ds(at, 16), :] = jnp.where(mixed_sign(hashed), -1.0, 1.0).astype(jnp.bfloat16)
        return carry

    lax.fori_loop(0, rows // 16, chunk, 0)


def make_signs(seed_and_col, feature_count, width, part, count, parts, table, deps):
    rows = 256
    steps = feature_count // parts // rows
    given = [] if table is None else [table]
    return pl.pallas_call(
        functools.partial(sign_kernel, part * (feature_count // parts)),
        grid=(steps * count,),
        out_shape=jax.ShapeDtypeStruct((feature_count, width), jnp.bfloat16),
        in_specs=[in_smem] + [anywhere] * (len(given) + len(deps)),
        out_specs=pl.BlockSpec((rows, width), lambda i: (i + part * steps, 0)),
        input_output_aliases={1: 0} if given else {},
        compiler_params=params,
        cost_estimate=cost(feature_count * width * 1200 * count // parts, feature_count * width),
        name="signs",
    )(seed_and_col, *given, *deps)


def curvature(gate_pre):
    sigmoid_val = jax.nn.sigmoid(gate_pre)
    return sigmoid_val * (1.0 - sigmoid_val) * (2.0 + gate_pre * (1.0 - 2.0 * sigmoid_val))


def stack(pieces, scratch):
    @pl.when(pl.program_id(0) == 0)
    def _():
        at = 0
        for piece in pieces:
            scratch[pl.ds(at, piece.shape[0]), :] = piece[...]
            at += piece.shape[0]


def factor_kernel(n_pieces, *refs):
    pieces = refs[:n_pieces]
    gate, up, sign = refs[n_pieces : n_pieces + 3]
    out, scratch = refs[-2:]
    stack(pieces, scratch)
    rows = scratch[...]
    gate_pre = jnp.dot(rows, gate[...], preferred_element_type=jnp.float32)
    up_proj = jnp.dot(rows, up[...], preferred_element_type=jnp.float32)
    tangent = jnp.dot(rows, sign[...], preferred_element_type=jnp.float32)
    out[...] = up_proj * curvature(gate_pre) * tangent


def make_factor(pieces, gate, up, signs, first, count, given, deps):
    depth, width = gate.shape
    block = column_block(width)
    rows = sum(p.shape[0] for p in pieces)
    n = len(pieces)
    given = [] if given is None else [given]
    weight = pl.BlockSpec((depth, block), lambda j: (0, j + first))
    return pl.pallas_call(
        functools.partial(factor_kernel, n),
        grid=(count,),
        out_shape=jax.ShapeDtypeStruct((rows, width), jnp.float32),
        in_specs=[pl.BlockSpec(p.shape, lambda j: (0, 0)) for p in pieces]
        + [weight] * 3
        + [anywhere] * (len(given) + len(deps)),
        out_specs=pl.BlockSpec((rows, block), lambda j: (0, j + first)),
        scratch_shapes=[pltpu.VMEM((rows, depth), jnp.bfloat16)],
        input_output_aliases={n + 3: 0} if given else {},
        compiler_params=params,
        cost_estimate=cost(6 * rows * depth * block * count, 6 * depth * block * count),
        name="factor",
    )(*pieces, gate, up, signs, *given, *deps)


def operand_kernel(n_pieces, n_deps, has_totals, *refs):
    pieces = refs[:n_pieces]
    down, factor = refs[n_pieces : n_pieces + 2]
    outs = refs[n_pieces + 2 + n_deps :]
    out, scratch, turned = outs[0], outs[-2], outs[-1]
    depth = down.shape[1]

    @pl.when(pl.program_id(0) == 0)
    def _():
        at = 0
        for piece in pieces:
            scratch[pl.ds(at, piece.shape[0]), :] = piece[:, :depth]
            at += piece.shape[0]
        turned[...] = scratch[...].T
        if has_totals:
            total = jnp.zeros((16, 128), jnp.float32)
            for piece in pieces:
                total += piece[:16, depth:].astype(jnp.float32)
            outs[1][...] = total

    back_grad = jnp.dot(down[...], turned[...], preferred_element_type=jnp.float32)
    out[...] = (back_grad.T * factor[...]).astype(jnp.bfloat16)


def make_operand(pieces, down, factor, first, count, has_totals, deps):
    width, depth = down.shape
    block = column_block(width)
    rows = factor.shape[0]
    n = len(pieces)
    out_shape = [jax.ShapeDtypeStruct((rows, block * count), jnp.bfloat16)]
    out_specs = [pl.BlockSpec((rows, block), lambda j: (0, j))]
    if has_totals:
        out_shape.append(jax.ShapeDtypeStruct((16, 128), jnp.float32))
        out_specs.append(pl.BlockSpec((16, 128), lambda j: (0, 0)))
    made = pl.pallas_call(
        functools.partial(operand_kernel, n, len(deps), has_totals),
        grid=(count,),
        out_shape=out_shape,
        in_specs=[pl.BlockSpec(p.shape, lambda j: (0, 0)) for p in pieces]
        + [
            pl.BlockSpec((block, depth), lambda j: (j + first, 0)),
            pl.BlockSpec((rows, block), lambda j: (0, j + first)),
        ]
        + [anywhere] * len(deps),
        out_specs=out_specs,
        scratch_shapes=[
            pltpu.VMEM((rows, depth), jnp.bfloat16),
            pltpu.VMEM((depth, rows), jnp.bfloat16),
        ],
        compiler_params=params,
        cost_estimate=cost(2 * rows * depth * block * count, 2 * depth * block * count),
        name="operand",
    )(*pieces, down, factor, *deps)
    return made if has_totals else (made[0], None)


def turn_kernel(*refs):
    out, scratch = refs[-2:]
    at = 0
    for part in refs[:-2]:
        scratch[pl.ds(at, part.shape[0]), :] = part[...]
        at += part.shape[0]
    out[...] = scratch[...].T


def turn_parts(parts):
    whole = pl.BlockSpec(memory_space=pltpu.VMEM)
    rows = sum(p.shape[0] for p in parts)
    cols = parts[0].shape[1]
    return pl.pallas_call(
        turn_kernel,
        out_shape=jax.ShapeDtypeStruct((cols, rows), jnp.bfloat16),
        in_specs=[whole] * len(parts),
        out_specs=whole,
        scratch_shapes=[pltpu.VMEM((rows, cols), jnp.bfloat16)],
        compiler_params=params,
        cost_estimate=cost(3e9, 4 * rows * cols),
        name="turn",
    )(*parts)


def hessian_kernel(n, finish, dp_ref, *refs):
    turned, operands = refs[0], refs[1 : n + 1]
    out, gathered = refs[-2:]
    at = 0
    for operand in operands:
        gathered[pl.ds(at, operand.shape[0]), :] = operand[...]
        at += operand.shape[0]
    total = jnp.dot(turned[...], gathered[...], preferred_element_type=jnp.float32)
    if finish:
        base, sign, totals = refs[n + 1 : n + 4]
        scale = 1.0 / totals[0:1, 0:1]
        total = (total + base[...]) * scale * sign[...].astype(jnp.float32)
    out[...] = total


def make_hessian(turned, operands, dp, first, width, finish, given, deps):
    out_rows, rows = turned.shape
    block = column_block(width)
    count = operands[0].shape[1] // block
    n = len(operands)
    given = [] if given is None else [given]
    extra_specs = [
        pl.BlockSpec((out_rows, block), lambda j, dp_ref: (0, j + first)),
        pl.BlockSpec((out_rows, block), lambda j, dp_ref: (dp_ref[0], j + first)),
        pl.BlockSpec((16, 128), lambda j, dp_ref: (0, 0)),
    ]
    return pl.pallas_call(
        functools.partial(hessian_kernel, n, bool(finish)),
        grid_spec=pltpu.PrefetchScalarGridSpec(
            num_scalar_prefetch=1,
            grid=(count,),
            in_specs=[pl.BlockSpec(turned.shape, lambda j, dp_ref: (0, 0))]
            + [pl.BlockSpec((o.shape[0], block), lambda j, dp_ref: (0, j)) for o in operands]
            + extra_specs[: len(finish)]
            + [anywhere] * (len(given) + len(deps)),
            out_specs=pl.BlockSpec((out_rows, block), lambda j, dp_ref: (0, j + first)),
            scratch_shapes=[pltpu.VMEM((rows, block), jnp.bfloat16)],
        ),
        out_shape=jax.ShapeDtypeStruct((out_rows, width), jnp.float32),
        input_output_aliases={n + 2 + len(finish): 0} if given else {},
        compiler_params=params,
        cost_estimate=cost(2 * rows * out_rows * block * count, 8 * out_rows * block * count),
        name="hessian",
    )(dp, turned, *operands, *finish, *given, *deps)


def nothing(*refs):
    pass


def after(value, deps):
    return pl.pallas_call(
        nothing,
        out_shape=jax.ShapeDtypeStruct(value.shape, value.dtype),
        in_specs=[anywhere] * (1 + len(deps)),
        out_specs=anywhere,
        input_output_aliases={0: 0},
        cost_estimate=cost(1e6, 1e3),
        name="after",
    )(value, *deps)


def take_kernel(n, at_ref, *refs):
    out, at = refs[-1], 0
    for piece in refs[:n]:
        out[pl.ds(at, piece.shape[0]), :] = piece[...]
        at += piece.shape[0]


def take_columns(pieces, at, width, deps):
    rows = sum(p.shape[0] for p in pieces)
    return pl.pallas_call(
        functools.partial(take_kernel, len(pieces)),
        grid_spec=pltpu.PrefetchScalarGridSpec(
            num_scalar_prefetch=1,
            grid=(1,),
            in_specs=[
                pl.BlockSpec((p.shape[0], width), lambda j, at_ref: (0, at_ref[0])) for p in pieces
            ]
            + [anywhere] * len(deps),
            out_specs=pl.BlockSpec((rows, width), lambda j, at_ref: (0, 0)),
        ),
        out_shape=jax.ShapeDtypeStruct((rows, width), pieces[0].dtype),
        compiler_params=params,
        cost_estimate=cost(2e9, 4 * rows * width),
        name="columns",
    )(at.astype(jnp.int32).reshape(1), *pieces, *deps)


def mask_kernel(rows, flags, *rest):
    rest[-1][...] = rows[...] * flags[...]


def masked_rows(rows, flags, deps):
    whole = pl.BlockSpec(memory_space=pltpu.VMEM)
    return pl.pallas_call(
        mask_kernel,
        out_shape=jax.ShapeDtypeStruct(rows.shape, rows.dtype),
        in_specs=[whole, whole] + [anywhere] * len(deps),
        out_specs=whole,
        compiler_params=params,
        name="masked",
    )(rows, jnp.broadcast_to(flags[:, None], rows.shape[:1] + (128,))[:, :1], *deps)


def ranks(mask, rows):
    before = lax.broadcasted_iota(jnp.int32, (rows, rows), 0) < lax.broadcasted_iota(
        jnp.int32, (rows, rows), 1
    )
    return jnp.dot(mask, before.astype(jnp.float32), preferred_element_type=jnp.float32)


def pack_kernel(rows, mask, kept, excess):
    size = rows.shape[0]
    live = mask[...].astype(jnp.float32)
    rank = ranks(live, size).astype(jnp.int32)
    slot = lax.broadcasted_iota(jnp.int32, (size, size), 0)
    pick = jnp.where((slot == rank) & (live > 0.5), 1.0, 0.0).astype(jnp.bfloat16)
    packed = jnp.dot(pick, rows[...], preferred_element_type=jnp.float32).astype(jnp.bfloat16)
    cap = kept.shape[0]
    kept[...] = packed[:cap]
    excess[...] = packed[cap:]


def pack_live(rows, mask, cap):
    whole = pl.BlockSpec(memory_space=pltpu.VMEM)
    return pl.pallas_call(
        pack_kernel,
        out_shape=[
            jax.ShapeDtypeStruct((cap, rows.shape[1]), rows.dtype),
            jax.ShapeDtypeStruct((rows.shape[0] - cap, rows.shape[1]), rows.dtype),
        ],
        in_specs=[whole, whole],
        out_specs=[whole, whole],
        compiler_params=params,
        cost_estimate=cost(2e9, 2 * rows.size * 2),
        name="pack",
    )(rows, mask)


def place_kernel(stat_in, *refs):
    kept, received, mask = refs[:3]
    out, left = refs[-2 - (not stat_in) :][:2]
    cap, more = kept.shape[0], received.shape[0]
    depth = kept.shape[1]
    live = jnp.sum(mask[...].astype(jnp.float32), axis=1, keepdims=True)
    first = jnp.minimum(live.astype(jnp.int32), cap)

    def moved(rows, start):
        slot = lax.broadcasted_iota(jnp.int32, (rows, more), 0) + start
        source = lax.broadcasted_iota(jnp.int32, (rows, more), 1) + first
        pick = jnp.where(slot == source, 1.0, 0.0).astype(jnp.bfloat16)
        return jnp.dot(pick, received[...], preferred_element_type=jnp.float32)

    rest = moved(more, cap)
    left[...] = rest.astype(jnp.bfloat16)
    out[:, :depth] = kept[...] + moved(cap, 0).astype(jnp.bfloat16)
    if stat_in:
        stat = refs[3]
        row = lax.broadcasted_iota(jnp.int32, (cap, 128), 0)
        lanes = jnp.where(row == 0, stat[0:1, :], jnp.where(row == 1, stat[1:2, :], 0.0))
        out[:, depth:] = lanes.astype(jnp.bfloat16)
    else:
        row = lax.broadcasted_iota(jnp.int32, (8, 128), 0)
        any_left = jnp.max(jnp.max(jnp.abs(rest), axis=1, keepdims=True), axis=0, keepdims=True)
        flag = jnp.where(any_left > 0.0, 1.0, 0.0)
        refs[-1][...] = jnp.where(row == 0, live, jnp.where(row == 1, flag, 0.0))


def place_rows(kept, received, mask, stat, deps):
    whole = pl.BlockSpec(memory_space=pltpu.VMEM)
    cap, depth = kept.shape
    given = [] if stat is None else [stat]
    out_shape = [
        jax.ShapeDtypeStruct((cap, depth + 128 * len(given)), kept.dtype),
        jax.ShapeDtypeStruct(received.shape, kept.dtype),
    ]
    if stat is None:
        out_shape.append(jax.ShapeDtypeStruct((8, 128), jnp.float32))
    return pl.pallas_call(
        functools.partial(place_kernel, stat is not None),
        out_shape=out_shape,
        in_specs=[whole] * (3 + len(given)) + [anywhere] * len(deps),
        out_specs=[whole] * len(out_shape),
        compiler_params=params,
        cost_estimate=cost(2e9, 2 * kept.size * 2),
        name="place",
    )(kept, received, mask, *given, *deps)


def sum_steps(value, axis):
    size = lax.axis_size(axis)
    if size & (size - 1):
        return [lax.psum(value, axis)]
    step, values = 1, []
    while step < size:
        value = value + lax.ppermute(value, axis, [(i, (i + step) % size) for i in range(size)])
        values.append(value)
        step *= 2
    return values


def gather_steps(piece, late):
    size = lax.axis_size("tensor")
    if size != 8:
        rows = lax.all_gather(piece, "tensor", axis=0, tiled=True)
        half = rows.shape[0] // 2
        return [rows[:half]], [rows[half:]], [[], [], []]
    step = [(i, (i + 2) % size) for i in range(size)]
    swap = [(i, i ^ 1) for i in range(size)]
    later = after(piece, late) if late else piece
    z = [piece]
    for k in range(3):
        z.append(lax.ppermute(z[-1] if k else later, "tensor", step))
    y = [lax.ppermute(p, "tensor", swap) for p in z[:3]]
    if late:
        y.append(lax.ppermute(later, "tensor", [(i, (i + 6) % size ^ 1) for i in range(size)]))
    else:
        y.append(lax.ppermute(z[3], "tensor", swap))
    marks = [[z[1], y[0]], [z[2], y[1]], [z[3], y[2]]]
    if late:
        marks[2] = [y[3]]
    return [z[0], y[0], z[1], y[1]], [z[2], y[2], z[3], y[3]], marks


def per_device(tokens, cotangent, loss_mask, gate_weight, up_weight, down_weight, probe_seed):
    depth, width = gate_weight.shape
    n_dp = lax.axis_size("dp")
    n_x = n_dp // 2
    out_rows = depth // n_dp
    dp = lax.axis_index("dp")
    first_col = lax.axis_index("tensor") * width
    seed_and_col = jnp.stack([probe_seed[0], first_col.astype(jnp.int32)])
    blocks = width // column_block(width)
    ends = [0, (blocks + 1) // 2, blocks]
    cuts = [(lo, hi - lo) for lo, hi in zip(ends, ends[1:]) if hi > lo]
    rows_dev = tokens.shape[0]
    cap = -(-3 * rows_dev // 64) * 16
    packing = cap < rows_dev and n_dp * rows_dev <= 256

    def move(i, j):
        return [(s, ((s // 2 + i) % n_x) * 2 + ((s % 2) ^ j)) for s in range(n_dp)]

    def spread_tokens(pieces, deps, later):
        def columns(piece, at, size):
            return lax.dynamic_slice_in_dim(piece, at, size, 1)

        chip, core = dp // 2, dp % 2
        received = []
        for i in range(1, n_x):
            sent = take_columns(pieces, (chip + i) % n_x, 2 * out_rows, deps)
            received.append(lax.ppermute(sent, "dp", move(i, 0)))

        if later:
            received = [after(r, later) for r in received]

        def of_core(c):
            return jnp.concatenate(
                [columns(p, (chip * 2 + c) * out_rows, out_rows) for p in pieces]
                + [columns(r, c * out_rows, out_rows) for r in received],
                axis=0,
            )

        return [of_core(core), lax.ppermute(of_core(1 - core), "dp", move(0, 1))]

    def spread_operand(operand, deps=()):
        parts = [lax.ppermute(operand, "dp", move(i, 0)) for i in range(1, n_x)]
        if deps:
            parts = [after(p, deps) for p in parts]
        parts = [operand] + parts
        return parts + [lax.ppermute(p, "dp", move(0, 1)) for p in parts]

    if packing:
        mirror = [(s, n_dp - 1 - s) for s in range(n_dp)]
        mask_row = loss_mask.reshape(1, rows_dev)
        kept, excess = pack_live(tokens, mask_row, cap)
        received = lax.ppermute(excess, "dp", mirror)
        kept_cot, excess_cot = pack_live(cotangent, mask_row, cap)
        received_cot = lax.ppermute(excess_cot, "dp", mirror)
        tokens, left, stat = place_rows(kept, received, mask_row, None, [])
    else:
        stat = jnp.zeros((8, 128), jnp.float32) + jnp.sum(loss_mask.astype(jnp.float32))
    stats = sum_steps(stat, "dp")
    early = [received_cot] if packing else []

    tok_a, tok_b, tok_marks = gather_steps(tokens, [])
    signs = None
    for first, count, deps in (
        (0, 1, [kept_cot] if packing else []),
        (1, 2, [tokens]),
        (3, 2, stats[:1] + early),
        (5, 3, tok_marks[0] + stats[-1:]),
    ):
        signs = make_signs(seed_and_col, depth, width, first, count, 8, signs, deps)
    if packing:
        masked, left_cot = place_rows(
            kept_cot, received_cot, mask_row, stats[-1], tok_marks[0]
        )
    else:
        masked = masked_rows(cotangent, loss_mask.astype(jnp.bfloat16), tok_marks[2])
    cot_a, cot_b, cot_marks = gather_steps(masked, tok_marks[2])

    def factor_of(tok, at, given, deps):
        if at >= len(cuts):
            return given
        first, count = cuts[at]
        return make_factor(tok, gate_weight, up_weight, signs, first, count, given, deps)

    factor_a = factor_of(tok_a, 0, None, tok_marks[1])
    factor_a = factor_of(tok_a, 1, factor_a, tok_marks[2] + cot_marks[0][1:])
    parts_a = spread_tokens(tok_a, [], [factor_a])
    factor_b = factor_of(tok_b, 0, None, cot_marks[0] + [factor_a])
    operand_a, totals = make_operand(
        cot_a, down_weight, factor_a, 0, blocks, packing, cot_marks[1] + parts_a + [factor_b]
    )
    parts_b = spread_tokens(tok_b, [factor_a], [operand_a])
    factor_b = factor_of(tok_b, 1, factor_b, [operand_a] + cot_marks[2])
    operands_a = spread_operand(operand_a, [factor_b])
    chunks, before = [], [operand_a, operands_a[n_x], parts_b[1]]
    for first, count in cuts:
        made, more = make_operand(
            cot_b, down_weight, factor_b, first, count, packing and first == 0, before
        )
        before = [made] + operands_a[1:]
        if more is not None:
            totals = totals + more
        chunks.append((first, made))
    if not packing:
        totals = jnp.zeros((16, 128), jnp.float32) + sum_steps(stats[-1], "tensor")[-1][0, 0]
    turned_a, turned_b = turn_parts(parts_a), turn_parts(parts_b)
    dp_at = dp.astype(jnp.int32).reshape(1)
    base = make_hessian(turned_a, operands_a, dp_at, 0, width, (), None, before)
    spread = [
        spread_operand(made, [] if k else [base]) for k, (first, made) in enumerate(chunks)
    ]
    out = None
    for (first, made), operands in zip(chunks, spread):
        others = [p[1] for p in spread if p is not operands] if out is None else []
        out = make_hessian(
            turned_b, operands, dp_at, first, width, (base, signs, totals), out, others
        )
    if not packing:
        return out

    def second_round(done):
        features = jnp.concatenate(sum(gather_steps(left, [])[:2], []), axis=0)
        rest = jnp.concatenate(sum(gather_steps(left_cot, [])[:2], []), axis=0)
        gate_pre = jnp.dot(features, gate_weight, preferred_element_type=jnp.float32)
        up_proj = jnp.dot(features, up_weight, preferred_element_type=jnp.float32)
        tangent = jnp.dot(features, signs, preferred_element_type=jnp.float32)
        back_grad = lax.dot_general(
            rest, down_weight, contract_last, preferred_element_type=jnp.float32
        )
        operand = (back_grad * up_proj * curvature(gate_pre) * tangent).astype(jnp.bfloat16)
        more = lax.dot_general(
            jnp.concatenate(spread_tokens([features], [], []), axis=0),
            jnp.concatenate(spread_operand(operand), axis=0),
            contract_rows,
            preferred_element_type=jnp.float32,
        )
        own_signs = lax.dynamic_slice_in_dim(signs, dp * out_rows, out_rows, 0)
        return done + more / totals[0, 0] * own_signs.astype(jnp.float32)

    return lax.cond(totals[1, 0] > 0.5, second_round, lambda done: done, out)


def solution(mesh):
    in_specs = (
        P(("dp", "tensor"), None),
        P(("dp", "tensor"), None),
        P(("dp", "tensor")),
        P(None, "tensor"),
        P(None, "tensor"),
        P("tensor", None),
        P(),
    )
    out_specs = P("dp", "tensor")
    return jax.shard_map(
        per_device, mesh=mesh, in_specs=in_specs, out_specs=out_specs, check_vma=False
    )
```

```python
import functools

import jax
import jax.numpy as jnp
from jax import lax
from jax.experimental import pallas as pl
from jax.experimental.pallas import tpu as pltpu
from jax.sharding import PartitionSpec as P

FF = 14336
MULT = -1640531535

contract_rows = (((0,), (0,)), ((), ()))
contract_last = (((1,), (1,)), ((), ()))

anywhere = pl.BlockSpec(memory_space=pl.ANY)
in_smem = pl.BlockSpec(memory_space=pltpu.SMEM)
params = pltpu.CompilerParams(vmem_limit_bytes=40 * 1024 * 1024)


def cost(flops, moved):
    return pl.CostEstimate(flops=int(flops), bytes_accessed=int(moved), transcendentals=0)


def mixed_sign(hashed):
    hashed = hashed ^ lax.shift_right_logical(hashed, jnp.full_like(hashed, 15))
    hashed = hashed * jnp.int32(739982445)
    hashed = hashed ^ lax.shift_right_logical(hashed, jnp.full_like(hashed, 12))
    hashed = hashed * jnp.int32(695872825)
    return (hashed ^ lax.shift_left(hashed, jnp.full_like(hashed, 15))) < 0


def column_block(width):
    return 256 if width % 256 == 0 else width


def sign_kernel(start_row, seed_and_col, *rest):
    out = rest[-1]
    rows, width = out.shape
    first = start_row + pl.program_id(0) * rows
    col = lax.broadcasted_iota(jnp.int32, (16, width), 1) + seed_and_col[1]
    row = lax.broadcasted_iota(jnp.int32, (16, width), 0)
    base = (row * FF + col) * jnp.int32(MULT) + seed_and_col[0] * jnp.int32(668265263)

    def chunk(c, carry):
        at = pl.multiple_of(c * 16, 16)
        hashed = base + (first + at) * (jnp.int32(FF) * jnp.int32(MULT))
        out[pl.ds(at, 16), :] = jnp.where(mixed_sign(hashed), -1.0, 1.0).astype(jnp.bfloat16)
        return carry

    lax.fori_loop(0, rows // 16, chunk, 0)


def make_signs(seed_and_col, feature_count, width, part, parts, table, deps):
    rows = 256
    steps = feature_count // parts // rows
    given = [] if table is None else [table]
    return pl.pallas_call(
        functools.partial(sign_kernel, part * (feature_count // parts)),
        grid=(steps,),
        out_shape=jax.ShapeDtypeStruct((feature_count, width), jnp.bfloat16),
        in_specs=[in_smem] + [anywhere] * (len(given) + len(deps)),
        out_specs=pl.BlockSpec((rows, width), lambda i: (i + part * steps, 0)),
        input_output_aliases={1: 0} if given else {},
        compiler_params=params,
        cost_estimate=cost(feature_count * width * 1200 // parts, feature_count * width),
        name="signs",
    )(seed_and_col, *given, *deps)


def curvature(gate_pre):
    sigmoid_val = jax.nn.sigmoid(gate_pre)
    return sigmoid_val * (1.0 - sigmoid_val) * (2.0 + gate_pre * (1.0 - 2.0 * sigmoid_val))


def stack(pieces, scratch):
    @pl.when(pl.program_id(0) == 0)
    def _():
        at = 0
        for piece in pieces:
            scratch[pl.ds(at, piece.shape[0]), :] = piece[...]
            at += piece.shape[0]


def factor_kernel(n_pieces, *refs):
    pieces = refs[:n_pieces]
    gate, up, sign = refs[n_pieces : n_pieces + 3]
    out, scratch = refs[-2:]
    stack(pieces, scratch)
    rows = scratch[...]
    gate_pre = jnp.dot(rows, gate[...], preferred_element_type=jnp.float32)
    up_proj = jnp.dot(rows, up[...], preferred_element_type=jnp.float32)
    tangent = jnp.dot(rows, sign[...], preferred_element_type=jnp.float32)
    out[...] = up_proj * curvature(gate_pre) * tangent


def make_factor(pieces, gate, up, signs, first, count, given, deps):
    depth, width = gate.shape
    block = column_block(width)
    rows = sum(p.shape[0] for p in pieces)
    n = len(pieces)
    given = [] if given is None else [given]
    weight = pl.BlockSpec((depth, block), lambda j: (0, j + first))
    return pl.pallas_call(
        functools.partial(factor_kernel, n),
        grid=(count,),
        out_shape=jax.ShapeDtypeStruct((rows, width), jnp.float32),
        in_specs=[pl.BlockSpec(p.shape, lambda j: (0, 0)) for p in pieces]
        + [weight] * 3
        + [anywhere] * (len(given) + len(deps)),
        out_specs=pl.BlockSpec((rows, block), lambda j: (0, j + first)),
        scratch_shapes=[pltpu.VMEM((rows, depth), jnp.bfloat16)],
        input_output_aliases={n + 3: 0} if given else {},
        compiler_params=params,
        cost_estimate=cost(6 * rows * depth * block * count, 6 * depth * block * count),
        name="factor",
    )(*pieces, gate, up, signs, *given, *deps)


def operand_kernel(n_pieces, n_deps, has_totals, *refs):
    pieces = refs[:n_pieces]
    down, factor = refs[n_pieces : n_pieces + 2]
    outs = refs[n_pieces + 2 + n_deps :]
    out, scratch, turned = outs[0], outs[-2], outs[-1]
    depth = down.shape[1]

    @pl.when(pl.program_id(0) == 0)
    def _():
        at = 0
        for piece in pieces:
            scratch[pl.ds(at, piece.shape[0]), :] = piece[:, :depth]
            at += piece.shape[0]
        turned[...] = scratch[...].T
        if has_totals:
            total = jnp.zeros((16, 128), jnp.float32)
            for piece in pieces:
                total += piece[:16, depth:].astype(jnp.float32)
            outs[1][...] = total

    back_grad = jnp.dot(down[...], turned[...], preferred_element_type=jnp.float32)
    out[...] = (back_grad.T * factor[...]).astype(jnp.bfloat16)


def make_operand(pieces, down, factor, first, count, has_totals, deps):
    width, depth = down.shape
    block = column_block(width)
    rows = factor.shape[0]
    n = len(pieces)
    out_shape = [jax.ShapeDtypeStruct((rows, block * count), jnp.bfloat16)]
    out_specs = [pl.BlockSpec((rows, block), lambda j: (0, j))]
    if has_totals:
        out_shape.append(jax.ShapeDtypeStruct((16, 128), jnp.float32))
        out_specs.append(pl.BlockSpec((16, 128), lambda j: (0, 0)))
    made = pl.pallas_call(
        functools.partial(operand_kernel, n, len(deps), has_totals),
        grid=(count,),
        out_shape=out_shape,
        in_specs=[pl.BlockSpec(p.shape, lambda j: (0, 0)) for p in pieces]
        + [
            pl.BlockSpec((block, depth), lambda j: (j + first, 0)),
            pl.BlockSpec((rows, block), lambda j: (0, j + first)),
        ]
        + [anywhere] * len(deps),
        out_specs=out_specs,
        scratch_shapes=[
            pltpu.VMEM((rows, depth), jnp.bfloat16),
            pltpu.VMEM((depth, rows), jnp.bfloat16),
        ],
        compiler_params=params,
        cost_estimate=cost(2 * rows * depth * block * count, 2 * depth * block * count),
        name="operand",
    )(*pieces, down, factor, *deps)
    return made if has_totals else (made[0], None)


def turn_kernel(*refs):
    out, scratch = refs[-2:]
    at = 0
    for part in refs[:-2]:
        scratch[pl.ds(at, part.shape[0]), :] = part[...]
        at += part.shape[0]
    out[...] = scratch[...].T


def turn_parts(parts):
    whole = pl.BlockSpec(memory_space=pltpu.VMEM)
    rows = sum(p.shape[0] for p in parts)
    cols = parts[0].shape[1]
    return pl.pallas_call(
        turn_kernel,
        out_shape=jax.ShapeDtypeStruct((cols, rows), jnp.bfloat16),
        in_specs=[whole] * len(parts),
        out_specs=whole,
        scratch_shapes=[pltpu.VMEM((rows, cols), jnp.bfloat16)],
        compiler_params=params,
        cost_estimate=cost(3e9, 4 * rows * cols),
        name="turn",
    )(*parts)


def hessian_kernel(n, finish, dp_ref, *refs):
    turned, operands = refs[0], refs[1 : n + 1]
    out, gathered = refs[-2:]
    at = 0
    for operand in operands:
        gathered[pl.ds(at, operand.shape[0]), :] = operand[...]
        at += operand.shape[0]
    total = jnp.dot(turned[...], gathered[...], preferred_element_type=jnp.float32)
    if finish:
        base, sign, totals = refs[n + 1 : n + 4]
        scale = 1.0 / totals[0:1, 0:1]
        total = (total + base[...]) * scale * sign[...].astype(jnp.float32)
    out[...] = total


def make_hessian(turned, operands, dp, first, width, finish, given, deps):
    out_rows, rows = turned.shape
    block = column_block(width)
    count = operands[0].shape[1] // block
    n = len(operands)
    given = [] if given is None else [given]
    extra_specs = [
        pl.BlockSpec((out_rows, block), lambda j, dp_ref: (0, j + first)),
        pl.BlockSpec((out_rows, block), lambda j, dp_ref: (dp_ref[0], j + first)),
        pl.BlockSpec((16, 128), lambda j, dp_ref: (0, 0)),
    ]
    return pl.pallas_call(
        functools.partial(hessian_kernel, n, bool(finish)),
        grid_spec=pltpu.PrefetchScalarGridSpec(
            num_scalar_prefetch=1,
            grid=(count,),
            in_specs=[pl.BlockSpec(turned.shape, lambda j, dp_ref: (0, 0))]
            + [pl.BlockSpec((o.shape[0], block), lambda j, dp_ref: (0, j)) for o in operands]
            + extra_specs[: len(finish)]
            + [anywhere] * (len(given) + len(deps)),
            out_specs=pl.BlockSpec((out_rows, block), lambda j, dp_ref: (0, j + first)),
            scratch_shapes=[pltpu.VMEM((rows, block), jnp.bfloat16)],
        ),
        out_shape=jax.ShapeDtypeStruct((out_rows, width), jnp.float32),
        input_output_aliases={n + 2 + len(finish): 0} if given else {},
        compiler_params=params,
        cost_estimate=cost(2 * rows * out_rows * block * count, 8 * out_rows * block * count),
        name="hessian",
    )(dp, turned, *operands, *finish, *given, *deps)


def nothing(*refs):
    pass


def after(value, deps):
    return pl.pallas_call(
        nothing,
        out_shape=jax.ShapeDtypeStruct(value.shape, value.dtype),
        in_specs=[anywhere] * (1 + len(deps)),
        out_specs=anywhere,
        input_output_aliases={0: 0},
        cost_estimate=cost(1e6, 1e3),
        name="after",
    )(value, *deps)


def take_kernel(n, at_ref, *refs):
    out, at = refs[-1], 0
    for piece in refs[:n]:
        out[pl.ds(at, piece.shape[0]), :] = piece[...]
        at += piece.shape[0]


def take_columns(pieces, at, width, deps):
    rows = sum(p.shape[0] for p in pieces)
    return pl.pallas_call(
        functools.partial(take_kernel, len(pieces)),
        grid_spec=pltpu.PrefetchScalarGridSpec(
            num_scalar_prefetch=1,
            grid=(1,),
            in_specs=[
                pl.BlockSpec((p.shape[0], width), lambda j, at_ref: (0, at_ref[0])) for p in pieces
            ]
            + [anywhere] * len(deps),
            out_specs=pl.BlockSpec((rows, width), lambda j, at_ref: (0, 0)),
        ),
        out_shape=jax.ShapeDtypeStruct((rows, width), pieces[0].dtype),
        compiler_params=params,
        cost_estimate=cost(2e9, 4 * rows * width),
        name="columns",
    )(at.astype(jnp.int32).reshape(1), *pieces, *deps)


def mask_kernel(rows, flags, *rest):
    rest[-1][...] = rows[...] * flags[...]


def masked_rows(rows, flags, deps):
    whole = pl.BlockSpec(memory_space=pltpu.VMEM)
    return pl.pallas_call(
        mask_kernel,
        out_shape=jax.ShapeDtypeStruct(rows.shape, rows.dtype),
        in_specs=[whole, whole] + [anywhere] * len(deps),
        out_specs=whole,
        compiler_params=params,
        name="masked",
    )(rows, jnp.broadcast_to(flags[:, None], rows.shape[:1] + (128,))[:, :1], *deps)


def ranks(mask, rows):
    before = lax.broadcasted_iota(jnp.int32, (rows, rows), 0) < lax.broadcasted_iota(
        jnp.int32, (rows, rows), 1
    )
    return jnp.dot(mask, before.astype(jnp.float32), preferred_element_type=jnp.float32)


def pack_kernel(rows, mask, kept, excess):
    size = rows.shape[0]
    live = mask[...].astype(jnp.float32)
    rank = ranks(live, size).astype(jnp.int32)
    slot = lax.broadcasted_iota(jnp.int32, (size, size), 0)
    pick = jnp.where((slot == rank) & (live > 0.5), 1.0, 0.0).astype(jnp.bfloat16)
    packed = jnp.dot(pick, rows[...], preferred_element_type=jnp.float32).astype(jnp.bfloat16)
    cap = kept.shape[0]
    kept[...] = packed[:cap]
    excess[...] = packed[cap:]


def pack_live(rows, mask, cap):
    whole = pl.BlockSpec(memory_space=pltpu.VMEM)
    return pl.pallas_call(
        pack_kernel,
        out_shape=[
            jax.ShapeDtypeStruct((cap, rows.shape[1]), rows.dtype),
            jax.ShapeDtypeStruct((rows.shape[0] - cap, rows.shape[1]), rows.dtype),
        ],
        in_specs=[whole, whole],
        out_specs=[whole, whole],
        compiler_params=params,
        cost_estimate=cost(2e9, 2 * rows.size * 2),
        name="pack",
    )(rows, mask)


def place_kernel(stat_in, *refs):
    kept, received, mask = refs[:3]
    out, left = refs[-2 - (not stat_in) :][:2]
    cap, more = kept.shape[0], received.shape[0]
    depth = kept.shape[1]
    live = jnp.sum(mask[...].astype(jnp.float32), axis=1, keepdims=True)
    first = jnp.minimum(live.astype(jnp.int32), cap)

    def moved(rows, start):
        slot = lax.broadcasted_iota(jnp.int32, (rows, more), 0) + start
        source = lax.broadcasted_iota(jnp.int32, (rows, more), 1) + first
        pick = jnp.where(slot == source, 1.0, 0.0).astype(jnp.bfloat16)
        return jnp.dot(pick, received[...], preferred_element_type=jnp.float32)

    rest = moved(more, cap)
    left[...] = rest.astype(jnp.bfloat16)
    out[:, :depth] = kept[...] + moved(cap, 0).astype(jnp.bfloat16)
    if stat_in:
        stat = refs[3]
        row = lax.broadcasted_iota(jnp.int32, (cap, 128), 0)
        lanes = jnp.where(row == 0, stat[0:1, :], jnp.where(row == 1, stat[1:2, :], 0.0))
        out[:, depth:] = lanes.astype(jnp.bfloat16)
    else:
        row = lax.broadcasted_iota(jnp.int32, (8, 128), 0)
        any_left = jnp.max(jnp.max(jnp.abs(rest), axis=1, keepdims=True), axis=0, keepdims=True)
        flag = jnp.where(any_left > 0.0, 1.0, 0.0)
        refs[-1][...] = jnp.where(row == 0, live, jnp.where(row == 1, flag, 0.0))


def place_rows(kept, received, mask, stat, deps):
    whole = pl.BlockSpec(memory_space=pltpu.VMEM)
    cap, depth = kept.shape
    given = [] if stat is None else [stat]
    out_shape = [
        jax.ShapeDtypeStruct((cap, depth + 128 * len(given)), kept.dtype),
        jax.ShapeDtypeStruct(received.shape, kept.dtype),
    ]
    if stat is None:
        out_shape.append(jax.ShapeDtypeStruct((8, 128), jnp.float32))
    return pl.pallas_call(
        functools.partial(place_kernel, stat is not None),
        out_shape=out_shape,
        in_specs=[whole] * (3 + len(given)) + [anywhere] * len(deps),
        out_specs=[whole] * len(out_shape),
        compiler_params=params,
        cost_estimate=cost(2e9, 2 * kept.size * 2),
        name="place",
    )(kept, received, mask, *given, *deps)


def sum_steps(value, axis):
    size = lax.axis_size(axis)
    if size & (size - 1):
        return [lax.psum(value, axis)]
    step, values = 1, []
    while step < size:
        value = value + lax.ppermute(value, axis, [(i, (i + step) % size) for i in range(size)])
        values.append(value)
        step *= 2
    return values


def gather_steps(piece, straight):
    size = lax.axis_size("tensor")
    if size != 8:
        rows = lax.all_gather(piece, "tensor", axis=0, tiled=True)
        half = rows.shape[0] // 2
        return [rows[:half]], [rows[half:]], [[], [], []]
    step = [(i, (i + 2) % size) for i in range(size)]
    swap = [(i, i ^ 1) for i in range(size)]
    z = [piece]
    for k in range(3):
        z.append(lax.ppermute(z[-1], "tensor", step))
    y = [lax.ppermute(p, "tensor", swap) for p in z[:3]]
    if straight:
        y.append(lax.ppermute(piece, "tensor", [(i, (i + 6) % size ^ 1) for i in range(size)]))
    else:
        y.append(lax.ppermute(z[3], "tensor", swap))
    marks = [[z[1], y[0]], [z[2], y[1]], [z[3], y[2]]]
    if straight:
        marks[2] = [y[3]]
    return [z[0], y[0], z[1], y[1]], [z[2], y[2], z[3], y[3]], marks


def per_device(tokens, cotangent, loss_mask, gate_weight, up_weight, down_weight, probe_seed):
    depth, width = gate_weight.shape
    n_dp = lax.axis_size("dp")
    n_x = n_dp // 2
    out_rows = depth // n_dp
    dp = lax.axis_index("dp")
    first_col = lax.axis_index("tensor") * width
    seed_and_col = jnp.stack([probe_seed[0], first_col.astype(jnp.int32)])
    blocks = width // column_block(width)
    ends = [0, (blocks + 1) // 2, blocks]
    cuts = [(lo, hi - lo) for lo, hi in zip(ends, ends[1:]) if hi > lo]
    rows_dev = tokens.shape[0]
    cap = -(-3 * rows_dev // 64) * 16
    packing = cap < rows_dev and n_dp * rows_dev <= 256

    def move(i, j):
        return [(s, ((s // 2 + i) % n_x) * 2 + ((s % 2) ^ j)) for s in range(n_dp)]

    def spread_tokens(pieces, deps):
        def columns(piece, at, size):
            return lax.dynamic_slice_in_dim(piece, at, size, 1)

        chip, core = dp // 2, dp % 2
        received = []
        for i in range(1, n_x):
            sent = take_columns(pieces, (chip + i) % n_x, 2 * out_rows, deps)
            received.append(lax.ppermute(sent, "dp", move(i, 0)))

        def of_core(c):
            return jnp.concatenate(
                [columns(p, (chip * 2 + c) * out_rows, out_rows) for p in pieces]
                + [columns(r, c * out_rows, out_rows) for r in received],
                axis=0,
            )

        return [of_core(core), lax.ppermute(of_core(1 - core), "dp", move(0, 1))]

    def spread_operand(operand, deps=()):
        parts = [lax.ppermute(operand, "dp", move(i, 0)) for i in range(1, n_x)]
        if deps:
            parts = [after(p, deps) for p in parts]
        parts = [operand] + parts
        return parts + [lax.ppermute(p, "dp", move(0, 1)) for p in parts]

    if packing:
        mirror = [(s, n_dp - 1 - s) for s in range(n_dp)]
        mask_row = loss_mask.reshape(1, rows_dev)
        kept, excess = pack_live(tokens, mask_row, cap)
        received = lax.ppermute(excess, "dp", mirror)
        kept_cot, excess_cot = pack_live(cotangent, mask_row, cap)
        received_cot = lax.ppermute(excess_cot, "dp", mirror)
        tokens, left, stat = place_rows(kept, received, mask_row, None, [])
    else:
        stat = jnp.zeros((8, 128), jnp.float32) + jnp.sum(loss_mask.astype(jnp.float32))
    stats = sum_steps(stat, "dp")
    early = [received_cot] if packing else []

    tok_a, tok_b, tok_marks = gather_steps(tokens, False)
    signs = make_signs(seed_and_col, depth, width, 0, 4, None, [tokens])
    signs = make_signs(seed_and_col, depth, width, 1, 4, signs, stats[:1] + early)
    signs = make_signs(seed_and_col, depth, width, 2, 4, signs, tok_marks[0] + stats[-1:])
    signs = make_signs(seed_and_col, depth, width, 3, 4, signs, [])
    if packing:
        masked, left_cot = place_rows(
            kept_cot, received_cot, mask_row, stats[-1], tok_marks[2] + [signs]
        )
    else:
        masked = masked_rows(cotangent, loss_mask.astype(jnp.bfloat16), tok_marks[2] + [signs])
    cot_a, cot_b, cot_marks = gather_steps(masked, True)
    parts_a = spread_tokens(tok_a, [])

    def factor_of(tok, at, given, deps):
        if at >= len(cuts):
            return given
        first, count = cuts[at]
        return make_factor(tok, gate_weight, up_weight, signs, first, count, given, deps)

    factor_a = factor_of(tok_a, 0, None, tok_marks[1])
    factor_a = factor_of(tok_a, 1, factor_a, tok_marks[2] + [masked])
    factor_b = factor_of(tok_b, 0, None, cot_marks[0][:1] + [factor_a])
    parts_b = spread_tokens(tok_b, [factor_b])
    operand_a, totals = make_operand(
        cot_a, down_weight, factor_a, 0, blocks, packing, cot_marks[1] + parts_a + [factor_b]
    )
    factor_b = factor_of(tok_b, 1, factor_b, [operand_a] + cot_b[1:3])
    operands_a = spread_operand(operand_a, [factor_b])
    chunks, before = [], [operand_a]
    for first, count in cuts:
        made, more = make_operand(
            cot_b, down_weight, factor_b, first, count, packing and first == 0, before
        )
        before = [made]
        if more is not None:
            totals = totals + more
        chunks.append((first, made))
    if not packing:
        totals = jnp.zeros((16, 128), jnp.float32) + sum_steps(stats[-1], "tensor")[-1][0, 0]
    turned_a, turned_b = turn_parts(parts_a), turn_parts(parts_b)
    dp_at = dp.astype(jnp.int32).reshape(1)
    base = make_hessian(turned_a, operands_a, dp_at, 0, width, (), None, before)
    spread = [
        spread_operand(made, [] if k else [base]) for k, (first, made) in enumerate(chunks)
    ]
    out = None
    for (first, made), operands in zip(chunks, spread):
        others = [p[1] for p in spread if p is not operands] if out is None else []
        out = make_hessian(
            turned_b, operands, dp_at, first, width, (base, signs, totals), out, others
        )
    if not packing:
        return out

    def second_round(done):
        features = jnp.concatenate(sum(gather_steps(left, False)[:2], []), axis=0)
        rest = jnp.concatenate(sum(gather_steps(left_cot, False)[:2], []), axis=0)
        gate_pre = jnp.dot(features, gate_weight, preferred_element_type=jnp.float32)
        up_proj = jnp.dot(features, up_weight, preferred_element_type=jnp.float32)
        tangent = jnp.dot(features, signs, preferred_element_type=jnp.float32)
        back_grad = lax.dot_general(
            rest, down_weight, contract_last, preferred_element_type=jnp.float32
        )
        operand = (back_grad * up_proj * curvature(gate_pre) * tangent).astype(jnp.bfloat16)
        more = lax.dot_general(
            jnp.concatenate(spread_tokens([features], []), axis=0),
            jnp.concatenate(spread_operand(operand), axis=0),
            contract_rows,
            preferred_element_type=jnp.float32,
        )
        own_signs = lax.dynamic_slice_in_dim(signs, dp * out_rows, out_rows, 0)
        return done + more / totals[0, 0] * own_signs.astype(jnp.float32)

    return lax.cond(totals[1, 0] > 0.5, second_round, lambda done: done, out)


def solution(mesh):
    in_specs = (
        P(("dp", "tensor"), None),
        P(("dp", "tensor"), None),
        P(("dp", "tensor")),
        P(None, "tensor"),
        P(None, "tensor"),
        P("tensor", None),
        P(),
    )
    out_specs = P("dp", "tensor")
    return jax.shard_map(
        per_device, mesh=mesh, in_specs=in_specs, out_specs=out_specs, check_vma=False
    )
```
